32 devices in a mesh: rep: 2 (over core), shard: 16 (over z, y, x).
Axes of the slice: x: 2, y: 2, z: 4, core: 2. Of those that a mesh axis runs over, the one named last changes fastest.
Arguments:
- tokens: bfloat16 [4096, 640], P(('rep', 'shard')), may hold values from -6 to 6
- lengths: int32 [32, 2], P(('rep', 'shard')), may hold values from 0 to 128, as said below
- w_query: bfloat16 [640, 1024], P('shard'), may hold values from -0.25 to 0.25
- w_key: bfloat16 [640, 256], P('shard'), may hold values from -0.25 to 0.25
- w_value: bfloat16 [640, 256], P('shard'), may hold values from -0.25 to 0.25
- w_out: bfloat16 [1024, 640], P('shard'), may hold values from -0.1875 to 0.1875
- w_gate: bfloat16 [640, 2048], P('shard'), may hold values from -0.25 to 0.25
- w_up: bfloat16 [640, 2048], P('shard'), may hold values from -0.25 to 0.25
- w_down: bfloat16 [2048, 640], P('shard'), may hold values from -0.125 to 0.125
- norm_gains: bfloat16 [4, 640], P(None, 'shard'), may hold values from 0.25 to 1.75
- head_gains: bfloat16 [2, 256], P(None, 'shard'), may hold values from 0.69921875 to 2
- cotangent: bfloat16 [4096, 640], P(('rep', 'shard')), may hold values from -6 to 6
Outputs:
- mixed: bfloat16 [4096, 640], P(('rep', 'shard'))
- tokens_grad: bfloat16 [4096, 640], P(('rep', 'shard'))
- w_query_grad: float32 [640, 1024], P('shard')
- w_key_grad: float32 [640, 256], P('shard')
- w_value_grad: float32 [640, 256], P('shard')
- w_out_grad: float32 [1024, 640], P('shard')
- w_gate_grad: float32 [640, 2048], P('shard')
- w_up_grad: float32 [640, 2048], P('shard')
- w_down_grad: float32 [2048, 640], P('shard')
- norm_gains_grad: float32 [4, 640], P(None, 'shard')
- head_gains_grad: float32 [2, 256], P(None, 'shard')
The draws below stay inside these ranges and needn't reach their ends.
Inputs may be any that keep to these rules, and one draw needn't show every extreme that they name: `lengths`: each row: first length at least 1, the two together between 64 and 128; in every draw one row holds a single sequence of 128 tokens and a second length of 0.
All inputs are finite; a program needn't handle non-finite values.
Results may differ from the reference program's by a relative error of at most 0.017.
Values may be sent and summed in bfloat16 or wider, within the bound.
A program may use at most 128 MiB of HBM per device.

```python
import math
from functools import partial
import jax
import jax.numpy as jnp
from jax import lax

D = 640
HQ = 4
HD = 256
FF = 2048
TOK_DEV = 128
HOLDERS = 32
TOKENS = 4096


def draw_lengths(key, part):
    key = jax.random.fold_in(key, 11)
    key_live, key_full, key_split = jax.random.split(key, 3)
    live_count = jax.random.randint(key_live, (HOLDERS,), TOK_DEV // 2, TOK_DEV + 1)
    full_holder = jax.random.randint(key_full, (), 0, HOLDERS)
    is_full = jnp.arange(HOLDERS, dtype=jnp.int32) == full_holder
    live_count = jnp.where(is_full, TOK_DEV, live_count)
    leading = 1 + jax.random.randint(key_split, (HOLDERS,), 0, 1 << 20) % live_count
    leading = jnp.where(is_full, TOK_DEV, leading)
    trailing = live_count - leading
    return jnp.stack([leading, trailing], axis=-1).astype(jnp.int32)


def block_levels(stream_key, shape, shards, low, high):
    def one(dim, shards_of):
        steps = jax.random.uniform(jax.random.fold_in(jax.random.fold_in(stream_key, 6), dim), (shards_of,), jnp.float32, low / len(shards), high / len(shards))
        return jnp.repeat(jnp.exp(steps), shape[dim] // shards_of).reshape((-1,) + (1,) * (len(shape) - dim - 1))

    loudness = one(*shards[0])
    for cut in shards[1:]:
        loudness = loudness * one(*cut)
    return loudness


def centred(rng, extent, width, most, cuts=(), kind=jnp.bfloat16):
    values = jax.random.normal(rng, extent, jnp.float32) * width
    if len(cuts) > 0:
        values = block_levels(rng, extent, cuts, -0.22, 0.18) * values
    return jnp.clip(values, min=-most, max=most).astype(kind)


def setup_inputs(seed: int = 0) -> dict:
    keys = jax.random.split(jax.random.key(seed), 13)
    tokens = centred(keys[0], (TOKENS, D), 1.0, 6.0, ((0, 32),))
    lengths = draw_lengths(jax.random.fold_in(keys[12], 71), 0)
    w_query = centred(keys[2], (D, HQ * HD), D ** -0.5, 0.25, ((0, 16),))
    w_key = centred(keys[3], (D, HD), D ** -0.5, 0.25, ((0, 16),))
    w_value = centred(keys[4], (D, HD), D ** -0.5, 0.25, ((0, 16),))
    w_out = centred(keys[5], (HQ * HD, D), (HQ * HD) ** -0.5, 0.1875, ((0, 16),))
    w_gate = centred(keys[6], (D, FF), D ** -0.5, 0.25, ((0, 16),))
    w_up = centred(keys[7], (D, FF), D ** -0.5, 0.25, ((0, 16),))
    w_down = centred(keys[8], (FF, D), FF ** -0.5, 0.125, ((0, 16),))
    norm_gains = jnp.clip(1.0 + 0.15 * jax.random.normal(keys[9], (4, D), jnp.float32), 0.25, 1.75).astype(jnp.bfloat16)
    head_gains = jnp.clip(jnp.exp(math.log(2.0) - 1.0509388 * jax.random.uniform(keys[10], (2, HD), jnp.float32) ** block_levels(keys[10], (2, HD), ((1, 16),), -0.2, 0.2)), 0.69921875, 2.0).astype(jnp.bfloat16)
    cotangent = centred(keys[11], (TOKENS, D), 1.0, 6.0, ((0, 32),))
    return {"tokens": tokens, "lengths": lengths, "w_query": w_query, "w_key": w_key, "w_value": w_value, "w_out": w_out, "w_gate": w_gate, "w_up": w_up, "w_down": w_down, "norm_gains": norm_gains, "head_gains": head_gains, "cotangent": cotangent}


EPSILON = 1e-06
THETA = 1000000.0
QUERY_SCALE = 0.0625

@jax.custom_vjp
def low(v):
    return lax.optimization_barrier(v.astype(jnp.bfloat16)).astype(jnp.float32)

@jax.custom_vjp
def low_back(v):
    return v

def low_keep(v):
    return (low(v), None)

def low_pass(kept, grad):
    return (grad,)

def back_keep(v):
    return (v, None)

def back_low(kept, grad):
    return (low(grad),)
low.defvjp(low_keep, low_pass)
low_back.defvjp(back_keep, back_low)

def rms_norm(values, gain_row):
    return values * lax.rsqrt(lax.optimization_barrier(jnp.mean(values * values, axis=-1, keepdims=True)) + EPSILON) * gain_row

def rotary(values, cos_part, sin_part):
    midway = values.shape[-1] // 2
    leading = values[..., :midway]
    second = values[..., midway:]
    return jnp.concatenate([leading * cos_part - second * sin_part, second * cos_part + leading * sin_part], axis=-1)

def layout(lengths, row_index):
    first_len = lengths[..., 0:1]
    second_len = lengths[..., 1:2]
    segment = (row_index >= first_len).astype(jnp.int32) + (row_index >= first_len + second_len).astype(jnp.int32)
    offset = jnp.where(segment == 0, 0, jnp.where(segment == 1, first_len, first_len + second_len)).astype(jnp.int32)
    return (segment, row_index - offset)

def angles(position, head_width):
    midway = head_width // 2
    frequency = jnp.exp(-(2.0 * jnp.arange(midway, dtype=jnp.float32) / head_width) * math.log(THETA))
    phase_angle = position.astype(jnp.float32)[..., None] * frequency
    return (jnp.cos(phase_angle), jnp.sin(phase_angle))

def mix(left, right):
    return jnp.dot(left, right, precision=lax.Precision.HIGHEST, preferred_element_type=jnp.float32)

def attend(inputs):
    query_block, key_block, value_block, segment = inputs
    row_index = jnp.arange(segment.shape[0], dtype=jnp.int32)
    scores = jnp.einsum('qhd,kd->hqk', query_block, key_block, precision=lax.Precision.HIGHEST)
    scores = low_back(scores)
    allowed = (segment[:, None] == segment[None, :]) & (row_index[None, :] <= row_index[:, None])
    scores = jnp.where(allowed[None], scores, -1e+30)
    top_score = lax.optimization_barrier(jnp.max(scores, axis=-1, keepdims=True))
    expo = jnp.exp(scores - top_score)
    probs = expo / lax.optimization_barrier(jnp.sum(expo, axis=-1, keepdims=True))
    return jnp.einsum('hqk,kd->qhd', low(probs), value_block, precision=lax.Precision.HIGHEST)

def forward(segment, position, live_mask, token_f32, w_query, w_key, w_value, w_out, w_gate, w_up, w_down, norm_gains, head_gains):
    cos_part, sin_part = angles(position, HD)
    normed_in = low(rms_norm(token_f32, norm_gains[0]))
    query_raw = low_back(mix(normed_in, w_query))
    key_raw = low_back(mix(normed_in, w_key))
    value_low = low_back(low(mix(normed_in, w_value)))
    query_heads = query_raw.reshape(TOKENS, HQ, HD)
    query_low = low(rotary(rms_norm(query_heads, head_gains[0]), cos_part[:, None, :], sin_part[:, None, :]) * QUERY_SCALE)
    key_low = low(rotary(rms_norm(key_raw, head_gains[1]), cos_part, sin_part))
    outputs = lax.map(jax.checkpoint(attend), (query_low.reshape(HOLDERS, TOK_DEV, HQ, HD), key_low.reshape(HOLDERS, TOK_DEV, HD), value_low.reshape(HOLDERS, TOK_DEV, HD), segment.reshape(HOLDERS, TOK_DEV)))
    attn_low = low_back(low(outputs.reshape(TOKENS, HQ * HD)))
    attn_proj = low_back(mix(attn_low, w_out))
    resid = token_f32 + rms_norm(attn_proj, norm_gains[1])
    normed_mid = low(rms_norm(resid, norm_gains[2]))
    gate_pre = low_back(mix(normed_mid, w_gate))
    up_pre = low_back(mix(normed_mid, w_up))
    act_low = low(jax.nn.gelu(gate_pre, approximate=True) * up_pre)
    down_out = low_back(mix(act_low, w_down))
    return (resid + rms_norm(down_out, norm_gains[3])) * live_mask[:, None]

def reference(tokens, lengths, w_query, w_key, w_value, w_out, w_gate, w_up, w_down, norm_gains, head_gains, cotangent):
    row_index = jnp.arange(TOK_DEV, dtype=jnp.int32)
    segment, position = layout(lengths, row_index)
    live_mask = (segment < 2).astype(jnp.float32).reshape(TOKENS)
    segment = segment.reshape(TOKENS)
    position = position.reshape(TOKENS)
    out, back = jax.vjp(partial(forward, segment, position, live_mask), tokens.astype(jnp.float32), w_query.astype(jnp.float32), w_key.astype(jnp.float32), w_value.astype(jnp.float32), w_out.astype(jnp.float32), w_gate.astype(jnp.float32), w_up.astype(jnp.float32), w_down.astype(jnp.float32), norm_gains.astype(jnp.float32), head_gains.astype(jnp.float32))
    grads = back(cotangent.astype(jnp.float32))
    return (out.astype(jnp.bfloat16), grads[0].astype(jnp.bfloat16), grads[1], grads[2], grads[3], grads[4], grads[5], grads[6], grads[7], grads[8], grads[9])
```

```python
from functools import partial
import math

import jax
import jax.numpy as jnp
from jax import lax
from jax.experimental import pallas as pl
from jax.experimental.pallas import tpu as pltpu
from jax.sharding import PartitionSpec as P

HQ = 4
HD = 256


EPSILON = 1e-06
THETA = 1000000.0
QUERY_SCALE = 0.0625


def rms_norm(values, gain_row):
    return (
        values * lax.rsqrt(jnp.mean(values * values, axis=-1, keepdims=True) + EPSILON) * gain_row
    )


def rotary(values, cos_part, sin_part):
    midway = values.shape[-1] // 2
    leading = values[..., :midway]
    second = values[..., midway:]
    return jnp.concatenate(
        [leading * cos_part - second * sin_part, second * cos_part + leading * sin_part], axis=-1
    )


def layout(lengths, row_index):
    first_len = lengths[..., 0:1]
    second_len = lengths[..., 1:2]
    segment = (row_index >= first_len).astype(jnp.int32) + (
        row_index >= first_len + second_len
    ).astype(jnp.int32)
    offset = jnp.where(segment == 0, 0, jnp.where(segment == 1, first_len, first_len + second_len))
    return (segment, row_index - offset)


def angles(position, head_width):
    midway = head_width // 2
    frequency = jnp.exp(
        -(2.0 * jnp.arange(midway, dtype=jnp.float32) / head_width) * math.log(THETA)
    )
    phase_angle = position.astype(jnp.float32)[..., None] * frequency
    return (jnp.cos(phase_angle), jnp.sin(phase_angle))


def lead_dot(left, right):
    return lax.dot_general(
        left, right, (((0,), (0,)), ((), ())), preferred_element_type=jnp.float32
    )


def tail_dot(left, right):
    return lax.dot_general(
        left, right, (((1,), (1,)), ((), ())), preferred_element_type=jnp.float32
    )


def prepare_heads(cos_part, sin_part, query_raw, key_raw, query_gain, key_gain):
    query_heads = query_raw.reshape(query_raw.shape[0], HQ, HD)
    query_rot = (
        rotary(rms_norm(query_heads, query_gain), cos_part[:, None, :], sin_part[:, None, :])
        * QUERY_SCALE
    )
    key_rot = rotary(rms_norm(key_raw, key_gain), cos_part, sin_part)
    return (query_rot, key_rot)


def middle(token_f32, attn_proj, post_gain, pre_gain):
    resid = token_f32 + rms_norm(attn_proj, post_gain)
    return (resid, rms_norm(resid, pre_gain))


def geglu(gate_pre, up_pre):
    return jax.nn.gelu(gate_pre, approximate=True) * up_pre


def finish(live_mask, resid, down_out, final_gain):
    return (resid + rms_norm(down_out, final_gain)) * live_mask[:, None]


def causal_mask(segment, row_index):
    return (segment[:, None] == segment[None, :]) & (row_index[None, :] <= row_index[:, None])


MESH = pl.DeviceIdType.MESH


def place():
    core = lax.axis_index("rep")
    me = lax.axis_index("shard")
    x = lax.rem(me, 2)
    y = lax.rem(me // 2, 2)
    z = me // 4

    def index(dz, first, second):
        flip_y = (1 - core) * first + core * second
        flip_x = core * first + (1 - core) * second
        ny = y + flip_y * (1 - 2 * y)
        nx = x + flip_x * (1 - 2 * x)
        return (lax.rem(z + dz, 4) * 2 + ny) * 2 + nx

    return core, me, index


def greet(core, me, index):
    barrier = pltpu.get_barrier_semaphore()
    partners = [(core, index(dz, 0, 0)) for dz in (1, 2, 3)]
    partners += [(core, index(0, 1, 0)), (core, index(0, 0, 1)), (1 - core, me)]
    for partner in partners:
        pl.semaphore_signal(barrier, inc=1, device_id=partner, device_id_type=MESH)
    pl.semaphore_wait(barrier, len(partners))


def gather_kernel(wide_in, tall_in, wide_out, tall_out, local_sem, send_sem, recv_sem):
    core, me, index = place()
    greet(core, me, index)
    pairs = ((wide_in, wide_out), (tall_in, tall_out))
    sent = []
    slot = [0]

    def send(block, target, own=False):
        for n, (source, dest) in enumerate(pairs):
            copy = pltpu.make_async_remote_copy(
                src_ref=source.at[core] if own else dest.at[core, block],
                dst_ref=dest.at[core, block],
                send_sem=send_sem.at[n, slot[0]],
                recv_sem=recv_sem.at[n, core, block],
                device_id=target,
                device_id_type=MESH,
            )
            copy.start()
            sent.append(copy)
        slot[0] += 1

    def arrive(half, block):
        for n, (_, dest) in enumerate(pairs):
            pltpu.make_async_remote_copy(
                src_ref=dest.at[half, block],
                dst_ref=dest.at[half, block],
                send_sem=send_sem.at[n, 0],
                recv_sem=recv_sem.at[n, half, block],
                device_id=(1 - core, me),
                device_id_type=MESH,
            ).wait_recv()

    first, second, other = (core, index(0, 1, 0)), (core, index(0, 0, 1)), (1 - core, me)
    for dz in (2, 1, 3):
        send(me, (core, index(dz, 0, 0)), True)
    send(me, second, True)
    send(me, first, True)
    kept = []
    for n, (source, dest) in enumerate(pairs):
        for half in (0, 1):
            copy = pltpu.make_async_copy(source.at[half], dest.at[half, me], local_sem.at[n, half])
            copy.start()
            kept.append(copy)
    ranks = (1, 3, 2)
    for dz in ranks:
        block = index(dz, 0, 0)
        arrive(core, block)
        send(block, second)
        send(block, first)
        send(block, other)
    for dz in (0,) + ranks:
        block = index(dz, 1, 0)
        arrive(core, block)
        send(block, second)
        send(block, other)
    for flip in (0, 1):
        for dz in (0,) + ranks:
            block = index(dz, flip, 1)
            arrive(core, block)
            send(block, other)
    for step in range(1, 16):
        arrive(1 - core, lax.rem(me + step, 16))
    for copy in kept:
        copy.wait()
    for copy in sent:
        copy.wait_send()


def gather_parts(wide, tall):
    return pl.pallas_call(
        gather_kernel,
        out_shape=(
            jax.ShapeDtypeStruct((2, 16) + wide.shape[1:], wide.dtype),
            jax.ShapeDtypeStruct((2, 16) + tall.shape[1:], tall.dtype),
        ),
        in_specs=[pl.BlockSpec(memory_space=pl.ANY)] * 2,
        out_specs=(pl.BlockSpec(memory_space=pl.ANY),) * 2,
        scratch_shapes=[
            pltpu.SemaphoreType.DMA((2, 2)),
            pltpu.SemaphoreType.DMA((2, 30)),
            pltpu.SemaphoreType.DMA((2, 2, 16)),
        ],
        compiler_params=pltpu.CompilerParams(collective_id=0, has_side_effects=True),
        name="gather_weights",
    )(wide, tall)


def scatter_kernel(wide_in, tall_in, wide_out, tall_out, *scratch):
    core, me, index = place()
    wide_buffers, tall_buffers = scratch[0:5], scratch[5:10]
    send_sem, recv_sem = scratch[10:12]
    greet(core, me, index)
    arrays = (
        (wide_in, wide_out) + tuple(wide_buffers),
        (tall_in, tall_out) + tuple(tall_buffers),
    )
    sent = []
    slot = [0]
    other = (1 - core, me)

    def send(pick_source, pick_dest, receive, target):
        for n, refs in enumerate(arrays):
            copy = pltpu.make_async_remote_copy(
                src_ref=pick_source(refs),
                dst_ref=pick_dest(refs),
                send_sem=send_sem.at[n, slot[0]],
                recv_sem=recv_sem.at[n, receive],
                device_id=target,
                device_id_type=MESH,
            )
            copy.start()
            sent.append(copy)
        slot[0] += 1

    def arrive(pick, receive):
        for n, refs in enumerate(arrays):
            pltpu.make_async_remote_copy(
                src_ref=pick(refs),
                dst_ref=pick(refs),
                send_sem=send_sem.at[n, 0],
                recv_sem=recv_sem.at[n, receive],
                device_id=other,
                device_id_type=MESH,
            ).wait_recv()

    order = (2, 1, 3, 0)
    position = 0
    for turned, straight in ((1, 0), (1, 1), (0, 1), (0, 0)):
        for dz in order:
            block = index(dz, turned, straight)
            send(
                lambda refs, block=block: refs[0].at[1 - core, block],
                lambda refs, at=position: refs[2].at[at],
                position,
                other,
            )
            position += 1

    position = 0
    for group, (turned, straight) in enumerate(((0, 1), (1, 1), (1, 0), (0, 0))):
        for rank, dz in enumerate(order):
            block = index(dz, turned, straight)
            incoming = [(2, position)]
            if group >= 2:
                incoming.append((3, {2: 4, 3: 0}[group] + rank))
            if group == 3:
                incoming.append((4, rank))
            bases = {2: 0, 3: 16, 4: 24, 5: 28}
            last = group == 3 and dz == 0
            if last:
                incoming += [(5, 0), (5, 1), (5, 2)]
            for which, at in incoming:
                arrive(lambda refs, which=which, at=at: refs[which].at[at], bases[which] + at)
            for refs in arrays:
                total = refs[0][core, block].astype(jnp.float32)
                for which, at in incoming:
                    total = total + refs[which][at].astype(jnp.float32)
                if last:
                    refs[1][core] = total.astype(jnp.bfloat16)
                else:
                    refs[6][position] = total.astype(jnp.bfloat16)
            source = lambda refs, at=position: refs[6].at[at]
            if group < 2:
                at = group * 4 + rank
                send(source, lambda refs, at=at: refs[3].at[at], 16 + at, (core, index(0, 0, 1)))
            elif group == 2:
                send(source, lambda refs, at=rank: refs[4].at[at], 24 + rank, (core, index(0, 1, 0)))
            elif not last:
                send(source, lambda refs, at=rank: refs[5].at[at], 28 + rank, (core, block))
            position += 1
    send(lambda refs: refs[1].at[core], lambda refs: refs[1].at[core], 31, other)
    arrive(lambda refs: refs[1].at[1 - core], 31)
    for copy in sent:
        copy.wait_send()


def scatter_parts(wide, tall):
    buffers = []
    for array in (wide, tall):
        for count in (16, 8, 4, 3, 15):
            buffers.append(pltpu.VMEM((count,) + array.shape[2:], array.dtype))
    return pl.pallas_call(
        scatter_kernel,
        out_shape=(
            jax.ShapeDtypeStruct((2,) + wide.shape[2:], wide.dtype),
            jax.ShapeDtypeStruct((2,) + tall.shape[2:], tall.dtype),
        ),
        in_specs=[pl.BlockSpec(memory_space=pltpu.VMEM)] * 2,
        out_specs=(pl.BlockSpec(memory_space=pltpu.VMEM),) * 2,
        scratch_shapes=buffers
        + [pltpu.SemaphoreType.DMA((2, 32)), pltpu.SemaphoreType.DMA((2, 32))],
        compiler_params=pltpu.CompilerParams(
            collective_id=1, has_side_effects=True, vmem_limit_bytes=52 * 1024 * 1024
        ),
        name="scatter_grads",
    )(wide, tall)


def halves(array, axis):
    size = array.shape[axis] // 2
    return (
        lax.slice_in_dim(array, 0, size, axis=axis),
        lax.slice_in_dim(array, size, 2 * size, axis=axis),
    )


def fill_row(values):
    flat = values.reshape(-1)
    return jnp.pad(flat[None], ((0, 15), (0, 640 - flat.shape[0])))


def gather_all(weights, norm_gains, head_gains):
    query, key, value, out, gate, up, down = weights
    columns = [halves(w, 1) for w in (query, key, value, gate, up)]
    wide = jnp.stack([jnp.concatenate([c[h] for c in columns], axis=1) for h in (0, 1)])
    rows = [halves(w, 0) for w in (out, down)]
    extra = (fill_row(norm_gains), fill_row(head_gains))
    tall = jnp.stack(
        [jnp.concatenate([r[h] for r in rows] + [extra[h]], axis=0) for h in (0, 1)]
    )
    wide, tall = gather_parts(wide, tall)
    wide = wide.reshape(2, 16 * wide.shape[2], wide.shape[3])
    spots = ((0, 512), (512, 640), (640, 768), (768, 1792), (1792, 2816))
    query, key, value, gate, up = (
        jnp.concatenate([wide[0, :, a:b], wide[1, :, a:b]], axis=1) for a, b in spots
    )
    out = jnp.concatenate([tall[0, :, :32], tall[1, :, :32]], axis=1).reshape(1024, 640)
    down = jnp.concatenate([tall[0, :, 32:96], tall[1, :, 32:96]], axis=1).reshape(2048, 640)
    norms = tall[0, :, 96, :160].reshape(16, 4, 40).transpose(1, 0, 2).reshape(4, 640)
    heads = tall[1, :, 96, :32].reshape(16, 2, 16).transpose(1, 0, 2).reshape(2, 256)
    return (query, key, value, out, gate, up, down, norms, heads)


def reduce_all(grads, norm_grad, head_grad):
    low = [g.astype(jnp.bfloat16) for g in grads]
    query, key, value, out, gate, up, down = low
    columns = [halves(w, 1) for w in (query, key, value, gate, up)]
    wide = jnp.stack([jnp.concatenate([c[h] for c in columns], axis=1) for h in (0, 1)])
    wide = wide.reshape(2, 16, 40, 2816)
    norm_low = norm_grad.astype(jnp.bfloat16).reshape(4, 16, 40).transpose(1, 0, 2).reshape(16, 160)
    head_low = head_grad.astype(jnp.bfloat16).reshape(2, 16, 16).transpose(1, 0, 2).reshape(16, 32)
    extra = (
        jnp.pad(norm_low[:, None], ((0, 0), (0, 15), (0, 480))),
        jnp.pad(head_low[:, None], ((0, 0), (0, 15), (0, 608))),
    )
    out = out.reshape(16, 64, 640)
    down = down.reshape(16, 128, 640)
    rows = [halves(w, 1) for w in (out, down)]
    tall = jnp.stack(
        [jnp.concatenate([r[h] for r in rows] + [extra[h]], axis=1) for h in (0, 1)]
    )
    wide, tall = scatter_parts(wide, tall)
    wide = wide.astype(jnp.float32)
    tall = tall.astype(jnp.float32)
    spots = ((0, 512), (512, 640), (640, 768), (768, 1792), (1792, 2816))
    query, key, value, gate, up = (
        jnp.concatenate([wide[0, :, a:b], wide[1, :, a:b]], axis=1) for a, b in spots
    )
    out = jnp.concatenate([tall[0, :32], tall[1, :32]], axis=0)
    down = jnp.concatenate([tall[0, 32:96], tall[1, 32:96]], axis=0)
    norms = tall[0, 96, :160].reshape(4, 40)
    heads = tall[1, 96, :32].reshape(2, 16)
    return (query, key, value, out, gate, up, down, norms, heads)


def gather_plain(weights, norm_gains, head_gains):
    full = tuple(lax.all_gather(w, "shard", axis=0, tiled=True) for w in weights)
    gains = tuple(
        lax.all_gather(g, "shard", axis=1, tiled=True) for g in (norm_gains, head_gains)
    )
    return full + gains


def reduce_plain(grads, norm_grad, head_grad):
    summed = tuple(
        lax.psum(lax.psum_scatter(g, "shard", scatter_dimension=0, tiled=True), "rep")
        for g in grads
    )
    gains = tuple(
        lax.psum(lax.psum_scatter(g, "shard", scatter_dimension=1, tiled=True), "rep")
        for g in (norm_grad, head_grad)
    )
    return summed + gains


def local(
    gather,
    reduce,
    tokens,
    lengths,
    w_query,
    w_key,
    w_value,
    w_out,
    w_gate,
    w_up,
    w_down,
    norm_gains,
    head_gains,
    cotangent,
):
    local_rows = tokens.shape[0]
    row_index = jnp.arange(local_rows, dtype=jnp.int32)
    segment, position = layout(lengths[0], row_index)
    live_mask = (segment < 2).astype(jnp.float32)
    cos_part, sin_part = angles(position, HD)
    gathered = gather(
        (w_query, w_key, w_value, w_out, w_gate, w_up, w_down), norm_gains, head_gains
    )
    (
        full_query,
        full_key,
        full_value,
        full_out,
        full_gate,
        full_up,
        full_down,
        full_norms,
        full_heads,
    ) = gathered
    gains = full_norms.astype(jnp.float32)
    head_scale = full_heads.astype(jnp.float32)
    token_f32 = tokens.astype(jnp.float32)
    normed_in, input_back = jax.vjp(rms_norm, token_f32, gains[0])
    input_low = normed_in.astype(jnp.bfloat16)
    query_raw = jnp.dot(input_low, full_query, preferred_element_type=jnp.float32)
    key_raw = jnp.dot(input_low, full_key, preferred_element_type=jnp.float32)
    value_low = jnp.dot(input_low, full_value, preferred_element_type=jnp.float32).astype(
        jnp.bfloat16
    )
    (query_rot, key_rot), heads_back = jax.vjp(
        partial(prepare_heads, cos_part, sin_part), query_raw, key_raw, head_scale[0], head_scale[1]
    )
    query_low = query_rot.astype(jnp.bfloat16)
    key_low = key_rot.astype(jnp.bfloat16)
    query_rows = query_low.transpose(1, 0, 2).reshape(HQ * local_rows, HD)
    scores = tail_dot(query_rows, key_low).reshape(HQ, local_rows, local_rows)
    scores = jnp.where(causal_mask(segment, row_index)[None], scores, -1e30)
    expo = jnp.exp(scores - jnp.max(scores, axis=-1, keepdims=True))
    probs = (expo / jnp.sum(expo, axis=-1, keepdims=True)).reshape(HQ * local_rows, local_rows)
    probs_low = probs.astype(jnp.bfloat16)
    outputs = jnp.dot(probs_low, value_low, preferred_element_type=jnp.float32)
    attn_low = (
        outputs.astype(jnp.bfloat16)
        .reshape(HQ, local_rows, HD)
        .transpose(1, 0, 2)
        .reshape(local_rows, HQ * HD)
    )
    attn_proj = jnp.dot(attn_low, full_out, preferred_element_type=jnp.float32)
    (resid, normed_mid), mid_back = jax.vjp(middle, token_f32, attn_proj, gains[1], gains[2])
    mid_low = normed_mid.astype(jnp.bfloat16)
    gate_pre = jnp.dot(mid_low, full_gate, preferred_element_type=jnp.float32)
    up_pre = jnp.dot(mid_low, full_up, preferred_element_type=jnp.float32)
    activated, glu_back = jax.vjp(geglu, gate_pre, up_pre)
    act_low = activated.astype(jnp.bfloat16)
    down_out = jnp.dot(act_low, full_down, preferred_element_type=jnp.float32)
    final, tail_back = jax.vjp(partial(finish, live_mask), resid, down_out, gains[3])
    mixed = final.astype(jnp.bfloat16)
    resid_grad, down_grad, final_gain_grad = tail_back(cotangent.astype(jnp.float32))
    down_low = down_grad.astype(jnp.bfloat16)
    grad_down = lead_dot(act_low, down_low)
    act_grad = tail_dot(down_low, full_down)
    gate_grad, up_grad = glu_back(act_grad)
    gate_low = gate_grad.astype(jnp.bfloat16)
    up_low = up_grad.astype(jnp.bfloat16)
    grad_gate = lead_dot(mid_low, gate_low)
    grad_up = lead_dot(mid_low, up_low)
    mid_grad = tail_dot(gate_low, full_gate) + tail_dot(up_low, full_up)
    token_grad_mid, attn_grad, post_gain_grad, pre_gain_grad = mid_back((resid_grad, mid_grad))
    attn_grad_low = attn_grad.astype(jnp.bfloat16)
    grad_out = lead_dot(attn_low, attn_grad_low)
    heads_grad = (
        tail_dot(attn_grad_low, full_out)
        .astype(jnp.bfloat16)
        .reshape(local_rows, HQ, HD)
        .transpose(1, 0, 2)
        .reshape(HQ * local_rows, HD)
    )
    value_grad = lead_dot(probs_low, heads_grad)
    prob_grad = tail_dot(heads_grad, value_low)
    score_grad = (probs * (prob_grad - jnp.sum(probs * prob_grad, axis=-1, keepdims=True))).astype(
        jnp.bfloat16
    )
    query_grad = jnp.dot(score_grad, key_low, preferred_element_type=jnp.float32)
    key_grad = lead_dot(score_grad, query_rows)
    query_grad = query_grad.reshape(HQ, local_rows, HD).transpose(1, 0, 2)
    query_raw_grad, key_raw_grad, query_gain_grad, key_gain_grad = heads_back(
        (query_grad, key_grad)
    )
    query_low_grad = query_raw_grad.astype(jnp.bfloat16)
    key_low_grad = key_raw_grad.astype(jnp.bfloat16)
    value_low_grad = value_grad.astype(jnp.bfloat16)
    grad_query = lead_dot(input_low, query_low_grad)
    grad_key = lead_dot(input_low, key_low_grad)
    grad_value = lead_dot(input_low, value_low_grad)
    input_grad = (
        tail_dot(query_low_grad, full_query)
        + tail_dot(key_low_grad, full_key)
        + tail_dot(value_low_grad, full_value)
    )
    token_grad_in, in_gain_grad = input_back(input_grad)
    tokens_grad = (token_grad_mid + token_grad_in).astype(jnp.bfloat16)
    norm_grad = jnp.stack([in_gain_grad, post_gain_grad, pre_gain_grad, final_gain_grad])
    head_grad = jnp.stack([query_gain_grad, key_gain_grad])
    results = reduce(
        (grad_query, grad_key, grad_value, grad_out, grad_gate, grad_up, grad_down),
        norm_grad,
        head_grad,
    )
    return (
        mixed,
        tokens_grad,
        results[0],
        results[1],
        results[2],
        results[3],
        results[4],
        results[5],
        results[6],
        results[7],
        results[8],
    )


def solution(mesh):
    if mesh.shape["rep"] == 2 and mesh.shape["shard"] == 16:
        steps = (gather_all, reduce_all)
    else:
        steps = (gather_plain, reduce_plain)
    placed = (
        P(("rep", "shard"), None),
        P(("rep", "shard"), None),
        P("shard", None),
        P("shard", None),
        P("shard", None),
        P("shard", None),
        P("shard", None),
        P("shard", None),
        P("shard", None),
        P(None, "shard"),
        P(None, "shard"),
        P(("rep", "shard"), None),
    )
    return jax.shard_map(
        partial(local, *steps),
        mesh=mesh,
        in_specs=placed,
        out_specs=(
            P(("rep", "shard"), None),
            P(("rep", "shard"), None),
            P("shard", None),
            P("shard", None),
            P("shard", None),
            P("shard", None),
            P("shard", None),
            P("shard", None),
            P("shard", None),
            P(None, "shard"),
            P(None, "shard"),
        ),
        check_vma=False,
    )
```

```python
from functools import partial
import math

import jax
import jax.numpy as jnp
from jax import lax
from jax.experimental import pallas as pl
from jax.experimental.pallas import tpu as pltpu
from jax.sharding import PartitionSpec as P

HQ = 4
HD = 256


EPSILON = 1e-06
THETA = 1000000.0
QUERY_SCALE = 0.0625


def rms_norm(values, gain_row):
    return (
        values * lax.rsqrt(jnp.mean(values * values, axis=-1, keepdims=True) + EPSILON) * gain_row
    )


def rotary(values, cos_part, sin_part):
    midway = values.shape[-1] // 2
    leading = values[..., :midway]
    second = values[..., midway:]
    return jnp.concatenate(
        [leading * cos_part - second * sin_part, second * cos_part + leading * sin_part], axis=-1
    )


def layout(lengths, row_index):
    first_len = lengths[..., 0:1]
    second_len = lengths[..., 1:2]
    segment = (row_index >= first_len).astype(jnp.int32) + (
        row_index >= first_len + second_len
    ).astype(jnp.int32)
    offset = jnp.where(segment == 0, 0, jnp.where(segment == 1, first_len, first_len + second_len))
    return (segment, row_index - offset)


def angles(position, head_width):
    midway = head_width // 2
    frequency = jnp.exp(
        -(2.0 * jnp.arange(midway, dtype=jnp.float32) / head_width) * math.log(THETA)
    )
    phase_angle = position.astype(jnp.float32)[..., None] * frequency
    return (jnp.cos(phase_angle), jnp.sin(phase_angle))


def lead_dot(left, right):
    return lax.dot_general(
        left, right, (((0,), (0,)), ((), ())), preferred_element_type=jnp.float32
    )


def tail_dot(left, right):
    return lax.dot_general(
        left, right, (((1,), (1,)), ((), ())), preferred_element_type=jnp.float32
    )


def double_dot(left, right_pair):
    left_pair = jnp.stack([left, left])
    return lax.dot_general(
        left_pair,
        jnp.stack([right_pair[0], right_pair[1]]),
        (((1,), (1,)), ((0,), (0,))),
        preferred_element_type=jnp.float32,
    ).astype(jnp.bfloat16)


def prepare_heads(cos_part, sin_part, query_raw, key_raw, query_gain, key_gain):
    query_heads = query_raw.reshape(query_raw.shape[0], HQ, HD)
    query_rot = (
        rotary(rms_norm(query_heads, query_gain), cos_part[:, None, :], sin_part[:, None, :])
        * QUERY_SCALE
    )
    key_rot = rotary(rms_norm(key_raw, key_gain), cos_part, sin_part)
    return (query_rot, key_rot)


def middle(token_f32, attn_proj, post_gain, pre_gain):
    resid = token_f32 + rms_norm(attn_proj, post_gain)
    return (resid, rms_norm(resid, pre_gain))


def geglu(gate_pre, up_pre):
    return jax.nn.gelu(gate_pre, approximate=True) * up_pre


def finish(live_mask, resid, down_out, final_gain):
    return (resid + rms_norm(down_out, final_gain)) * live_mask[:, None]


def causal_mask(segment, row_index):
    return (segment[:, None] == segment[None, :]) & (row_index[None, :] <= row_index[:, None])


MESH = pl.DeviceIdType.MESH


def place():
    core = lax.axis_index("rep")
    me = lax.axis_index("shard")
    x = lax.rem(me, 2)
    y = lax.rem(me // 2, 2)
    z = me // 4

    def index(dz, first, second):
        flip_y = (1 - core) * first + core * second
        flip_x = core * first + (1 - core) * second
        ny = y + flip_y * (1 - 2 * y)
        nx = x + flip_x * (1 - 2 * x)
        return (lax.rem(z + dz, 4) * 2 + ny) * 2 + nx

    return core, me, index


def greet(core, me, index):
    barrier = pltpu.get_barrier_semaphore()
    partners = [(core, index(dz, 0, 0)) for dz in (1, 2, 3)]
    partners += [(core, index(0, 1, 0)), (core, index(0, 0, 1)), (1 - core, me)]
    for partner in partners:
        pl.semaphore_signal(barrier, inc=1, device_id=partner, device_id_type=MESH)
    pl.semaphore_wait(barrier, len(partners))


def gather_kernel(*refs):
    local_sem, send_sem, recv_sem = refs[-3:]
    count = (len(refs) - 3) // 2
    core, me, index = place()
    greet(core, me, index)
    pairs = tuple(zip(refs[:count], refs[count : 2 * count]))
    sent = []
    slot = [0]

    def send(block, target, own=False):
        for n, (source, dest) in enumerate(pairs):
            copy = pltpu.make_async_remote_copy(
                src_ref=source.at[core] if own else dest.at[core, block],
                dst_ref=dest.at[core, block],
                send_sem=send_sem.at[n, slot[0]],
                recv_sem=recv_sem.at[n, core, block],
                device_id=target,
                device_id_type=MESH,
            )
            copy.start()
            sent.append(copy)
        slot[0] += 1

    def arrive(half, block):
        for n, (_, dest) in enumerate(pairs):
            pltpu.make_async_remote_copy(
                src_ref=dest.at[half, block],
                dst_ref=dest.at[half, block],
                send_sem=send_sem.at[n, 0],
                recv_sem=recv_sem.at[n, half, block],
                device_id=(1 - core, me),
                device_id_type=MESH,
            ).wait_recv()

    first, second, other = (core, index(0, 1, 0)), (core, index(0, 0, 1)), (1 - core, me)
    for dz in (2, 1, 3):
        send(me, (core, index(dz, 0, 0)), True)
    send(me, second, True)
    send(me, first, True)
    kept = []
    for n, (source, dest) in enumerate(pairs):
        for half in (0, 1):
            copy = pltpu.make_async_copy(source.at[half], dest.at[half, me], local_sem.at[n, half])
            copy.start()
            kept.append(copy)
    ranks = (1, 3, 2)
    for dz in ranks:
        block = index(dz, 0, 0)
        arrive(core, block)
        send(block, second)
        send(block, first)
        send(block, other)
    for dz in (0,) + ranks:
        block = index(dz, 1, 0)
        arrive(core, block)
        send(block, second)
        send(block, other)
    for flip in (0, 1):
        for dz in (0,) + ranks:
            block = index(dz, flip, 1)
            arrive(core, block)
            send(block, other)
    for step in range(1, 16):
        arrive(1 - core, lax.rem(me + step, 16))
    for copy in kept:
        copy.wait()
    for copy in sent:
        copy.wait_send()


def gather_parts(*arrays):
    count = len(arrays)
    return pl.pallas_call(
        gather_kernel,
        out_shape=tuple(jax.ShapeDtypeStruct((2, 16) + a.shape[1:], a.dtype) for a in arrays),
        in_specs=[pl.BlockSpec(memory_space=pl.ANY)] * count,
        out_specs=(pl.BlockSpec(memory_space=pl.ANY),) * count,
        scratch_shapes=[
            pltpu.SemaphoreType.DMA((count, 2)),
            pltpu.SemaphoreType.DMA((count, 30)),
            pltpu.SemaphoreType.DMA((count, 2, 16)),
        ],
        compiler_params=pltpu.CompilerParams(collective_id=0, has_side_effects=True),
        name="gather_weights",
    )(*arrays)


def scatter_kernel(*refs):
    core, me, index = place()
    send_sem, recv_sem = refs[-2:]
    count = (len(refs) - 2) // 7
    scratch = refs[2 * count : -2]
    greet(core, me, index)
    arrays = tuple(
        (refs[n], refs[count + n]) + tuple(scratch[5 * n : 5 * n + 5]) for n in range(count)
    )
    sent = []
    slot = [0]
    other = (1 - core, me)

    def send(pick_source, pick_dest, receive, target):
        for n, refs in enumerate(arrays):
            copy = pltpu.make_async_remote_copy(
                src_ref=pick_source(refs),
                dst_ref=pick_dest(refs),
                send_sem=send_sem.at[n, slot[0]],
                recv_sem=recv_sem.at[n, receive],
                device_id=target,
                device_id_type=MESH,
            )
            copy.start()
            sent.append(copy)
        slot[0] += 1

    def arrive(pick, receive):
        for n, refs in enumerate(arrays):
            pltpu.make_async_remote_copy(
                src_ref=pick(refs),
                dst_ref=pick(refs),
                send_sem=send_sem.at[n, 0],
                recv_sem=recv_sem.at[n, receive],
                device_id=other,
                device_id_type=MESH,
            ).wait_recv()

    order = (2, 1, 3, 0)
    position = 0
    for turned, straight in ((1, 1), (1, 0), (0, 1), (0, 0)):
        for dz in order:
            block = index(dz, turned, straight)
            send(
                lambda refs, block=block: refs[0].at[1 - core, block],
                lambda refs, at=position: refs[2].at[at],
                position,
                other,
            )
            position += 1

    position = 0
    for group, (turned, straight) in enumerate(((1, 1), (0, 1), (1, 0), (0, 0))):
        for rank, dz in enumerate(order):
            block = index(dz, turned, straight)
            incoming = [(2, position)]
            if group >= 2:
                incoming.append((3, (group - 2) * 4 + rank))
            if group == 3:
                incoming.append((4, rank))
            bases = {2: 0, 3: 16, 4: 24, 5: 28}
            last = group == 3 and dz == 0
            if last:
                incoming += [(5, 0), (5, 1), (5, 2)]
            for which, at in incoming:
                arrive(lambda refs, which=which, at=at: refs[which].at[at], bases[which] + at)
            for refs in arrays:
                total = refs[0][core, block].astype(jnp.float32)
                for which, at in incoming:
                    total = total + refs[which][at].astype(jnp.float32)
                if last:
                    refs[1][core] = total.astype(jnp.bfloat16)
                else:
                    refs[6][position] = total.astype(jnp.bfloat16)
            source = lambda refs, at=position: refs[6].at[at]
            if group < 2:
                at = group * 4 + rank
                send(source, lambda refs, at=at: refs[3].at[at], 16 + at, (core, index(0, 0, 1)))
            elif group == 2:
                send(source, lambda refs, at=rank: refs[4].at[at], 24 + rank, (core, index(0, 1, 0)))
            elif not last:
                send(source, lambda refs, at=rank: refs[5].at[at], 28 + rank, (core, block))
            position += 1
    send(lambda refs: refs[1].at[core], lambda refs: refs[1].at[core], 31, other)
    arrive(lambda refs: refs[1].at[1 - core], 31)
    for copy in sent:
        copy.wait_send()


def scatter_parts(*arrays):
    count = len(arrays)
    buffers = []
    for array in arrays:
        for slots in (16, 8, 4, 3, 15):
            buffers.append(pltpu.VMEM((slots,) + array.shape[2:], array.dtype))
    return pl.pallas_call(
        scatter_kernel,
        out_shape=tuple(jax.ShapeDtypeStruct((2,) + a.shape[2:], a.dtype) for a in arrays),
        in_specs=[pl.BlockSpec(memory_space=pltpu.VMEM)] * count,
        out_specs=(pl.BlockSpec(memory_space=pltpu.VMEM),) * count,
        scratch_shapes=buffers
        + [pltpu.SemaphoreType.DMA((count, 32)), pltpu.SemaphoreType.DMA((count, 32))],
        compiler_params=pltpu.CompilerParams(
            collective_id=1, has_side_effects=True, vmem_limit_bytes=52 * 1024 * 1024
        ),
        name="scatter_grads",
    )(*arrays)


def pair(*columns):
    return jnp.stack(
        [
            jnp.concatenate(
                [c[:, h * c.shape[1] // 2 : (h + 1) * c.shape[1] // 2] for c in columns], axis=1
            )
            for h in (0, 1)
        ]
    )


def unpair(both, start, size):
    return jnp.concatenate(
        [both[h, :, start : start + size] for h in (0, 1)], axis=1
    )


def gather_all(weights, norm_gains, head_gains):
    query, key, value, out, gate, up, down = weights
    gains = jnp.pad(norm_gains.T, ((0, 0), (0, 124))) + jnp.pad(
        head_gains.T, ((0, 24), (4, 122))
    )
    front = pair(query, key, value, jnp.concatenate([gains, gains], axis=1))
    front, wide, tall, high = gather_parts(
        front, pair(gate, up), out.reshape(2, 32, 640), down.reshape(2, 64, 640)
    )
    out = jnp.swapaxes(tall, 0, 1).reshape(1024, 640)
    down = jnp.swapaxes(high, 0, 1).reshape(2048, 640)
    norms = front[0, :, :, 768:772].reshape(640, 4).T
    heads = front[0, :, :16, 772:774].reshape(256, 2).T
    return (front.reshape(2, 640, 896), out, wide.reshape(2, 640, 2048), down, norms, heads)


def gather_plain(weights, norm_gains, head_gains):
    query, key, value, out, gate, up, down = (
        lax.all_gather(w, "shard", axis=0, tiled=True) for w in weights
    )
    norms, heads = (
        lax.all_gather(g, "shard", axis=1, tiled=True) for g in (norm_gains, head_gains)
    )
    blank = jnp.zeros((query.shape[0], 256), query.dtype)
    return (pair(query, key, value, blank), out, pair(gate, up), down, norms, heads)


def reduce_all(front, out, wide, down, norm_grad, head_grad):
    gains = jnp.pad(norm_grad.T, ((0, 0), (0, 124))) + jnp.pad(
        jnp.pad(head_grad.T.reshape(16, 16, 2), ((0, 0), (0, 24), (0, 0))).reshape(640, 2),
        ((0, 0), (4, 122)),
    )
    gains = gains.astype(jnp.bfloat16)
    front = lax.dynamic_update_slice(front, gains[None], (0, 0, 768))
    tall = jnp.swapaxes(out.reshape(16, 2, 32, 640), 0, 1)
    high = jnp.swapaxes(down.reshape(16, 2, 64, 640), 0, 1)
    summed = scatter_parts(
        front.reshape(2, 16, 40, 896), tall, wide.reshape(2, 16, 40, 2048), high
    )
    front, tall, wide, high = (v.astype(jnp.float32) for v in summed)
    return (
        unpair(front, 0, 512),
        unpair(front, 512, 128),
        unpair(front, 640, 128),
        tall.reshape(64, 640),
        unpair(wide, 0, 1024),
        unpair(wide, 1024, 1024),
        high.reshape(128, 640),
        front[0, :, 768:772].T,
        front[0, :16, 772:774].T,
    )


def reduce_plain(front, out, wide, down, norm_grad, head_grad):
    grads = (
        unpair(front, 0, 512),
        unpair(front, 512, 128),
        unpair(front, 640, 128),
        out,
        unpair(wide, 0, 1024),
        unpair(wide, 1024, 1024),
        down,
    )
    summed = tuple(
        lax.psum(
            lax.psum_scatter(g.astype(jnp.float32), "shard", scatter_dimension=0, tiled=True),
            "rep",
        )
        for g in grads
    )
    gains = tuple(
        lax.psum(lax.psum_scatter(g, "shard", scatter_dimension=1, tiled=True), "rep")
        for g in (norm_grad, head_grad)
    )
    return summed + gains


def local(
    gather,
    reduce,
    tokens,
    lengths,
    w_query,
    w_key,
    w_value,
    w_out,
    w_gate,
    w_up,
    w_down,
    norm_gains,
    head_gains,
    cotangent,
):
    local_rows = tokens.shape[0]
    row_index = jnp.arange(local_rows, dtype=jnp.int32)
    segment, position = layout(lengths[0], row_index)
    live_mask = (segment < 2).astype(jnp.float32)
    cos_part, sin_part = angles(position, HD)
    gathered = gather(
        (w_query, w_key, w_value, w_out, w_gate, w_up, w_down), norm_gains, head_gains
    )
    front, full_out, wide, full_down, full_norms, full_heads = gathered
    gains = full_norms.astype(jnp.float32)
    head_scale = full_heads.astype(jnp.float32)
    token_f32 = tokens.astype(jnp.float32)
    normed_in, input_back = jax.vjp(rms_norm, token_f32, gains[0])
    input_low = normed_in.astype(jnp.bfloat16)
    raw = [jnp.dot(input_low, front[h], preferred_element_type=jnp.float32) for h in (0, 1)]
    query_raw = jnp.concatenate([r[:, :512] for r in raw], axis=1)
    key_raw = jnp.concatenate([r[:, 512:640] for r in raw], axis=1)
    value_low = jnp.concatenate([r[:, 640:768] for r in raw], axis=1).astype(jnp.bfloat16)
    (query_rot, key_rot), heads_back = jax.vjp(
        partial(prepare_heads, cos_part, sin_part), query_raw, key_raw, head_scale[0], head_scale[1]
    )
    query_low = query_rot.astype(jnp.bfloat16)
    key_low = key_rot.astype(jnp.bfloat16)
    query_rows = query_low.transpose(1, 0, 2).reshape(HQ * local_rows, HD)
    scores = tail_dot(query_rows, key_low).reshape(HQ, local_rows, local_rows)
    scores = jnp.where(causal_mask(segment, row_index)[None], scores, -1e30)
    expo = jnp.exp(scores - jnp.max(scores, axis=-1, keepdims=True))
    probs = (expo / jnp.sum(expo, axis=-1, keepdims=True)).reshape(HQ * local_rows, local_rows)
    probs_low = probs.astype(jnp.bfloat16)
    outputs = jnp.dot(probs_low, value_low, preferred_element_type=jnp.float32)
    attn_low = (
        outputs.astype(jnp.bfloat16)
        .reshape(HQ, local_rows, HD)
        .transpose(1, 0, 2)
        .reshape(local_rows, HQ * HD)
    )
    attn_proj = jnp.dot(attn_low, full_out, preferred_element_type=jnp.float32)
    (resid, normed_mid), mid_back = jax.vjp(middle, token_f32, attn_proj, gains[1], gains[2])
    mid_low = normed_mid.astype(jnp.bfloat16)
    pre = [jnp.dot(mid_low, wide[h], preferred_element_type=jnp.float32) for h in (0, 1)]
    hidden = pre[0].shape[1] // 2
    glu = [jax.vjp(geglu, p[:, :hidden], p[:, hidden:]) for p in pre]
    act_low = jnp.concatenate([act.astype(jnp.bfloat16) for act, _ in glu], axis=1)
    down_out = jnp.dot(act_low, full_down, preferred_element_type=jnp.float32)
    final, tail_back = jax.vjp(partial(finish, live_mask), resid, down_out, gains[3])
    mixed = final.astype(jnp.bfloat16)
    resid_grad, down_grad, final_gain_grad = tail_back(cotangent.astype(jnp.float32))
    down_low = down_grad.astype(jnp.bfloat16)
    grad_down = lead_dot(act_low, down_low).astype(jnp.bfloat16)
    act_grad = tail_dot(down_low, full_down)
    pre_low = []
    for h, (_, glu_back) in enumerate(glu):
        parts = glu_back(act_grad[:, h * hidden : (h + 1) * hidden])
        pre_low.append(jnp.concatenate([g.astype(jnp.bfloat16) for g in parts], axis=1))
    grad_wide = double_dot(mid_low, pre_low)
    mid_grad = tail_dot(pre_low[0], wide[0]) + tail_dot(pre_low[1], wide[1])
    token_grad_mid, attn_grad, post_gain_grad, pre_gain_grad = mid_back((resid_grad, mid_grad))
    attn_grad_low = attn_grad.astype(jnp.bfloat16)
    grad_out = lead_dot(attn_low, attn_grad_low).astype(jnp.bfloat16)
    heads_grad = (
        tail_dot(attn_grad_low, full_out)
        .astype(jnp.bfloat16)
        .reshape(local_rows, HQ, HD)
        .transpose(1, 0, 2)
        .reshape(HQ * local_rows, HD)
    )
    value_grad = lead_dot(probs_low, heads_grad)
    prob_grad = tail_dot(heads_grad, value_low)
    score_grad = (probs * (prob_grad - jnp.sum(probs * prob_grad, axis=-1, keepdims=True))).astype(
        jnp.bfloat16
    )
    query_grad = jnp.dot(score_grad, key_low, preferred_element_type=jnp.float32)
    key_grad = lead_dot(score_grad, query_rows)
    query_grad = query_grad.reshape(HQ, local_rows, HD).transpose(1, 0, 2)
    query_raw_grad, key_raw_grad, query_gain_grad, key_gain_grad = heads_back(
        (query_grad, key_grad)
    )
    query_low_grad = query_raw_grad.astype(jnp.bfloat16)
    key_low_grad = key_raw_grad.astype(jnp.bfloat16)
    value_low_grad = value_grad.astype(jnp.bfloat16)
    blank = jnp.zeros((local_rows, 256), jnp.bfloat16)
    raw_low = pair(query_low_grad, key_low_grad, value_low_grad, blank)
    grad_front = double_dot(input_low, raw_low)
    input_grad = tail_dot(raw_low[0], front[0]) + tail_dot(raw_low[1], front[1])
    token_grad_in, in_gain_grad = input_back(input_grad)
    tokens_grad = (token_grad_mid + token_grad_in).astype(jnp.bfloat16)
    norm_grad = jnp.stack([in_gain_grad, post_gain_grad, pre_gain_grad, final_gain_grad])
    head_grad = jnp.stack([query_gain_grad, key_gain_grad])
    results = reduce(grad_front, grad_out, grad_wide, grad_down, norm_grad, head_grad)
    return (
        mixed,
        tokens_grad,
        results[0],
        results[1],
        results[2],
        results[3],
        results[4],
        results[5],
        results[6],
        results[7],
        results[8],
    )


def solution(mesh):
    if mesh.shape["rep"] == 2 and mesh.shape["shard"] == 16:
        steps = (gather_all, reduce_all)
    else:
        steps = (gather_plain, reduce_plain)
    placed = (
        P(("rep", "shard"), None),
        P(("rep", "shard"), None),
        P("shard", None),
        P("shard", None),
        P("shard", None),
        P("shard", None),
        P("shard", None),
        P("shard", None),
        P("shard", None),
        P(None, "shard"),
        P(None, "shard"),
        P(("rep", "shard"), None),
    )
    return jax.shard_map(
        partial(local, *steps),
        mesh=mesh,
        in_specs=placed,
        out_specs=(
            P(("rep", "shard"), None),
            P(("rep", "shard"), None),
            P("shard", None),
            P("shard", None),
            P("shard", None),
            P("shard", None),
            P("shard", None),
            P("shard", None),
            P("shard", None),
            P(None, "shard"),
            P(None, "shard"),
        ),
        check_vma=False,
    )
```

```python
from functools import partial
import math

import jax
import jax.numpy as jnp
from jax import lax
from jax.experimental import pallas as pl
from jax.experimental.pallas import tpu as pltpu
from jax.sharding import PartitionSpec as P

HQ = 4
HD = 256


EPSILON = 1e-06
THETA = 1000000.0
QUERY_SCALE = 0.0625


def rms_norm(values, gain_row):
    return (
        values * lax.rsqrt(jnp.mean(values * values, axis=-1, keepdims=True) + EPSILON) * gain_row
    )


def rotary(values, cos_part, sin_part):
    midway = values.shape[-1] // 2
    leading = values[..., :midway]
    second = values[..., midway:]
    return jnp.concatenate(
        [leading * cos_part - second * sin_part, second * cos_part + leading * sin_part], axis=-1
    )


def layout(lengths, row_index):
    first_len = lengths[..., 0:1]
    second_len = lengths[..., 1:2]
    segment = (row_index >= first_len).astype(jnp.int32) + (
        row_index >= first_len + second_len
    ).astype(jnp.int32)
    offset = jnp.where(segment == 0, 0, jnp.where(segment == 1, first_len, first_len + second_len))
    return (segment, row_index - offset)


def angles(position, head_width):
    midway = head_width // 2
    frequency = jnp.exp(
        -(2.0 * jnp.arange(midway, dtype=jnp.float32) / head_width) * math.log(THETA)
    )
    phase_angle = position.astype(jnp.float32)[..., None] * frequency
    return (jnp.cos(phase_angle), jnp.sin(phase_angle))


def lead_dot(left, right):
    return lax.dot_general(
        left, right, (((0,), (0,)), ((), ())), preferred_element_type=jnp.float32
    )


def tail_dot(left, right):
    return lax.dot_general(
        left, right, (((1,), (1,)), ((), ())), preferred_element_type=jnp.float32
    )


def double_dot(left, right_pair):
    left_pair = jnp.stack([left, left])
    return lax.dot_general(
        left_pair,
        jnp.stack([right_pair[0], right_pair[1]]),
        (((1,), (1,)), ((0,), (0,))),
        preferred_element_type=jnp.float32,
    ).astype(jnp.bfloat16)


def prepare_heads(cos_part, sin_part, query_raw, key_raw, query_gain, key_gain):
    query_heads = query_raw.reshape(query_raw.shape[0], HQ, HD)
    query_rot = (
        rotary(rms_norm(query_heads, query_gain), cos_part[:, None, :], sin_part[:, None, :])
        * QUERY_SCALE
    )
    key_rot = rotary(rms_norm(key_raw, key_gain), cos_part, sin_part)
    return (query_rot, key_rot)


def middle(token_f32, attn_proj, post_gain, pre_gain):
    resid = token_f32 + rms_norm(attn_proj, post_gain)
    return (resid, rms_norm(resid, pre_gain))


def geglu(gate_pre, up_pre):
    return jax.nn.gelu(gate_pre, approximate=True) * up_pre


def finish(live_mask, resid, down_out, final_gain):
    return (resid + rms_norm(down_out, final_gain)) * live_mask[:, None]


def causal_mask(segment, row_index):
    return (segment[:, None] == segment[None, :]) & (row_index[None, :] <= row_index[:, None])


MESH = pl.DeviceIdType.MESH


def place():
    core = lax.axis_index("rep")
    me = lax.axis_index("shard")
    x = lax.rem(me, 2)
    y = lax.rem(me // 2, 2)
    z = me // 4

    def index(dz, first, second):
        flip_y = (1 - core) * first + core * second
        flip_x = core * first + (1 - core) * second
        ny = y + flip_y * (1 - 2 * y)
        nx = x + flip_x * (1 - 2 * x)
        return (lax.rem(z + dz, 4) * 2 + ny) * 2 + nx

    return core, me, index


def greet(core, me, index):
    barrier = pltpu.get_barrier_semaphore()
    partners = [(core, index(dz, 0, 0)) for dz in (1, 2, 3)]
    partners += [(core, index(0, 1, 0)), (core, index(0, 0, 1)), (1 - core, me)]
    for partner in partners:
        pl.semaphore_signal(barrier, inc=1, device_id=partner, device_id_type=MESH)
    pl.semaphore_wait(barrier, len(partners))


def gather_kernel(*refs):
    local_sem, send_sem, recv_sem = refs[-3:]
    count = (len(refs) - 3) // 2
    core, me, index = place()
    greet(core, me, index)
    pairs = tuple(zip(refs[:count], refs[count : 2 * count]))
    sent = []
    slot = [0]

    def send(block, target, own=False):
        for n, (source, dest) in enumerate(pairs):
            copy = pltpu.make_async_remote_copy(
                src_ref=source.at[core] if own else dest.at[core, block],
                dst_ref=dest.at[core, block],
                send_sem=send_sem.at[n, slot[0]],
                recv_sem=recv_sem.at[n, core, block],
                device_id=target,
                device_id_type=MESH,
            )
            copy.start()
            sent.append(copy)
        slot[0] += 1

    def arrive(half, block):
        for n, (_, dest) in enumerate(pairs):
            pltpu.make_async_remote_copy(
                src_ref=dest.at[half, block],
                dst_ref=dest.at[half, block],
                send_sem=send_sem.at[n, 0],
                recv_sem=recv_sem.at[n, half, block],
                device_id=(1 - core, me),
                device_id_type=MESH,
            ).wait_recv()

    first, second, other = (core, index(0, 1, 0)), (core, index(0, 0, 1)), (1 - core, me)
    for dz in (2, 1, 3):
        send(me, (core, index(dz, 0, 0)), True)
    send(me, second, True)
    send(me, first, True)
    kept = []
    for n, (source, dest) in enumerate(pairs):
        for half in (0, 1):
            copy = pltpu.make_async_copy(source.at[half], dest.at[half, me], local_sem.at[n, half])
            copy.start()
            kept.append(copy)
    ranks = (1, 3, 2)
    for dz in ranks:
        block = index(dz, 0, 0)
        arrive(core, block)
        send(block, second)
        send(block, first)
        send(block, other)
    for dz in (0,) + ranks:
        block = index(dz, 1, 0)
        arrive(core, block)
        send(block, second)
        send(block, other)
    for flip in (0, 1):
        for dz in (0,) + ranks:
            block = index(dz, flip, 1)
            arrive(core, block)
            send(block, other)
    for step in range(1, 16):
        arrive(1 - core, lax.rem(me + step, 16))
    for copy in kept:
        copy.wait()
    for copy in sent:
        copy.wait_send()


def gather_parts(*arrays):
    count = len(arrays)
    return pl.pallas_call(
        gather_kernel,
        out_shape=tuple(jax.ShapeDtypeStruct((2, 16) + a.shape[1:], a.dtype) for a in arrays),
        in_specs=[pl.BlockSpec(memory_space=pl.ANY)] * count,
        out_specs=(pl.BlockSpec(memory_space=pl.ANY),) * count,
        scratch_shapes=[
            pltpu.SemaphoreType.DMA((count, 2)),
            pltpu.SemaphoreType.DMA((count, 30)),
            pltpu.SemaphoreType.DMA((count, 2, 16)),
        ],
        compiler_params=pltpu.CompilerParams(collective_id=0, has_side_effects=True),
        name="gather_weights",
    )(*arrays)


def scatter_kernel(*refs):
    core, me, index = place()
    send_sem, recv_sem = refs[-2:]
    count = (len(refs) - 2) // 7
    scratch = refs[2 * count : -2]
    greet(core, me, index)
    arrays = tuple(
        (refs[n], refs[count + n]) + tuple(scratch[5 * n : 5 * n + 5]) for n in range(count)
    )
    sent = []
    slot = [0]
    other = (1 - core, me)

    def send(pick_source, pick_dest, receive, target):
        for n, refs in enumerate(arrays):
            copy = pltpu.make_async_remote_copy(
                src_ref=pick_source(refs),
                dst_ref=pick_dest(refs),
                send_sem=send_sem.at[n, slot[0]],
                recv_sem=recv_sem.at[n, receive],
                device_id=target,
                device_id_type=MESH,
            )
            copy.start()
            sent.append(copy)
        slot[0] += 1

    def arrive(pick, receive):
        for n, refs in enumerate(arrays):
            pltpu.make_async_remote_copy(
                src_ref=pick(refs),
                dst_ref=pick(refs),
                send_sem=send_sem.at[n, 0],
                recv_sem=recv_sem.at[n, receive],
                device_id=other,
                device_id_type=MESH,
            ).wait_recv()

    order = (2, 1, 3, 0)
    position = 0
    for turned, straight in ((1, 1), (1, 0), (0, 1), (0, 0)):
        for dz in order:
            block = index(dz, turned, straight)
            send(
                lambda refs, block=block: refs[0].at[1 - core, block],
                lambda refs, at=position: refs[2].at[at],
                position,
                other,
            )
            position += 1

    position = 0
    for group, (turned, straight) in enumerate(((1, 1), (0, 1), (1, 0), (0, 0))):
        for rank, dz in enumerate(order):
            block = index(dz, turned, straight)
            incoming = [(2, position)]
            if group >= 2:
                incoming.append((3, (group - 2) * 4 + rank))
            if group == 3:
                incoming.append((4, rank))
            bases = {2: 0, 3: 16, 4: 24, 5: 28}
            last = group == 3 and dz == 0
            if last:
                incoming += [(5, 0), (5, 1), (5, 2)]
            for which, at in incoming:
                arrive(lambda refs, which=which, at=at: refs[which].at[at], bases[which] + at)
            for refs in arrays:
                total = refs[0][core, block].astype(jnp.float32)
                for which, at in incoming:
                    total = total + refs[which][at].astype(jnp.float32)
                if last:
                    refs[1][core] = total.astype(jnp.bfloat16)
                else:
                    refs[6][position] = total.astype(jnp.bfloat16)
            source = lambda refs, at=position: refs[6].at[at]
            if group < 2:
                at = group * 4 + rank
                send(source, lambda refs, at=at: refs[3].at[at], 16 + at, (core, index(0, 0, 1)))
            elif group == 2:
                send(source, lambda refs, at=rank: refs[4].at[at], 24 + rank, (core, index(0, 1, 0)))
            elif not last:
                send(source, lambda refs, at=rank: refs[5].at[at], 28 + rank, (core, block))
            position += 1
    send(lambda refs: refs[1].at[core], lambda refs: refs[1].at[core], 31, other)
    arrive(lambda refs: refs[1].at[1 - core], 31)
    for copy in sent:
        copy.wait_send()


def scatter_parts(*arrays):
    count = len(arrays)
    buffers = []
    for array in arrays:
        for slots in (16, 8, 4, 3, 15):
            buffers.append(pltpu.VMEM((slots,) + array.shape[2:], array.dtype))
    return pl.pallas_call(
        scatter_kernel,
        out_shape=tuple(jax.ShapeDtypeStruct((2,) + a.shape[2:], a.dtype) for a in arrays),
        in_specs=[pl.BlockSpec(memory_space=pltpu.VMEM)] * count,
        out_specs=(pl.BlockSpec(memory_space=pltpu.VMEM),) * count,
        scratch_shapes=buffers
        + [pltpu.SemaphoreType.DMA((count, 32)), pltpu.SemaphoreType.DMA((count, 32))],
        compiler_params=pltpu.CompilerParams(
            collective_id=1, has_side_effects=True, vmem_limit_bytes=52 * 1024 * 1024
        ),
        name="scatter_grads",
    )(*arrays)


def pair(*columns):
    return jnp.stack(
        [
            jnp.concatenate(
                [c[:, h * c.shape[1] // 2 : (h + 1) * c.shape[1] // 2] for c in columns], axis=1
            )
            for h in (0, 1)
        ]
    )


def unpair(both, start, size):
    return jnp.concatenate(
        [both[h, :, start : start + size] for h in (0, 1)], axis=1
    )


def gather_all(weights, norm_gains, head_gains):
    query, key, value, out, gate, up, down = weights
    gains = jnp.pad(norm_gains.T, ((0, 0), (0, 124))) + jnp.pad(
        head_gains.T, ((0, 24), (4, 122))
    )
    front = pair(query, key, value, jnp.concatenate([gains, gains], axis=1))
    front, wide, tall, high = gather_parts(
        front, pair(gate, up), out.reshape(2, 32, 640), down.reshape(2, 64, 640)
    )
    norms = front[0, :, :, 768:772].reshape(640, 4).T
    heads = front[0, :, :16, 772:774].reshape(256, 2).T
    return (front.reshape(2, 640, 896), tall, wide.reshape(2, 640, 2048), high, norms, heads)


def gather_plain(weights, norm_gains, head_gains):
    query, key, value, out, gate, up, down = (
        lax.all_gather(w, "shard", axis=0, tiled=True) for w in weights
    )
    norms, heads = (
        lax.all_gather(g, "shard", axis=1, tiled=True) for g in (norm_gains, head_gains)
    )
    blank = jnp.zeros((query.shape[0], 256), query.dtype)
    return (pair(query, key, value, blank), out, pair(gate, up), down, norms, heads)


def reduce_all(front, tall, wide, high, norm_grad, head_grad):
    gains = jnp.pad(norm_grad.T, ((0, 0), (0, 124))) + jnp.pad(
        jnp.pad(head_grad.T.reshape(16, 16, 2), ((0, 0), (0, 24), (0, 0))).reshape(640, 2),
        ((0, 0), (4, 122)),
    )
    gains = gains.astype(jnp.bfloat16)
    front = lax.dynamic_update_slice(front, gains[None], (0, 0, 768))
    summed = scatter_parts(
        front.reshape(2, 16, 40, 896), tall, wide.reshape(2, 16, 40, 2048), high
    )
    front, tall, wide, high = (v.astype(jnp.float32) for v in summed)
    return (
        unpair(front, 0, 512),
        unpair(front, 512, 128),
        unpair(front, 640, 128),
        tall.reshape(64, 640),
        unpair(wide, 0, 1024),
        unpair(wide, 1024, 1024),
        high.reshape(128, 640),
        front[0, :, 768:772].T,
        front[0, :16, 772:774].T,
    )


def reduce_plain(front, out, wide, down, norm_grad, head_grad):
    grads = (
        unpair(front, 0, 512),
        unpair(front, 512, 128),
        unpair(front, 640, 128),
        out,
        unpair(wide, 0, 1024),
        unpair(wide, 1024, 1024),
        down,
    )
    summed = tuple(
        lax.psum(
            lax.psum_scatter(g.astype(jnp.float32), "shard", scatter_dimension=0, tiled=True),
            "rep",
        )
        for g in grads
    )
    gains = tuple(
        lax.psum(lax.psum_scatter(g, "shard", scatter_dimension=1, tiled=True), "rep")
        for g in (norm_grad, head_grad)
    )
    return summed + gains


def local(
    gather,
    reduce,
    tokens,
    lengths,
    w_query,
    w_key,
    w_value,
    w_out,
    w_gate,
    w_up,
    w_down,
    norm_gains,
    head_gains,
    cotangent,
):
    local_rows = tokens.shape[0]
    row_index = jnp.arange(local_rows, dtype=jnp.int32)
    segment, position = layout(lengths[0], row_index)
    live_mask = (segment < 2).astype(jnp.float32)
    cos_part, sin_part = angles(position, HD)
    gathered = gather(
        (w_query, w_key, w_value, w_out, w_gate, w_up, w_down), norm_gains, head_gains
    )
    front, full_out, wide, full_down, full_norms, full_heads = gathered
    gains = full_norms.astype(jnp.float32)
    head_scale = full_heads.astype(jnp.float32)
    token_f32 = tokens.astype(jnp.float32)
    normed_in, input_back = jax.vjp(rms_norm, token_f32, gains[0])
    input_low = normed_in.astype(jnp.bfloat16)
    raw = [jnp.dot(input_low, front[h], preferred_element_type=jnp.float32) for h in (0, 1)]
    query_raw = jnp.concatenate([r[:, :512] for r in raw], axis=1)
    key_raw = jnp.concatenate([r[:, 512:640] for r in raw], axis=1)
    value_low = jnp.concatenate([r[:, 640:768] for r in raw], axis=1).astype(jnp.bfloat16)
    (query_rot, key_rot), heads_back = jax.vjp(
        partial(prepare_heads, cos_part, sin_part), query_raw, key_raw, head_scale[0], head_scale[1]
    )
    query_low = query_rot.astype(jnp.bfloat16)
    key_low = key_rot.astype(jnp.bfloat16)
    query_rows = query_low.transpose(1, 0, 2).reshape(HQ * local_rows, HD)
    scores = tail_dot(query_rows, key_low).reshape(HQ, local_rows, local_rows)
    scores = jnp.where(causal_mask(segment, row_index)[None], scores, -1e30)
    expo = jnp.exp(scores - jnp.max(scores, axis=-1, keepdims=True))
    probs = (expo / jnp.sum(expo, axis=-1, keepdims=True)).reshape(HQ * local_rows, local_rows)
    probs_low = probs.astype(jnp.bfloat16)
    outputs = jnp.dot(probs_low, value_low, preferred_element_type=jnp.float32)
    attn_low = (
        outputs.astype(jnp.bfloat16)
        .reshape(HQ, local_rows, HD)
        .transpose(1, 0, 2)
        .reshape(local_rows, HQ * HD)
    )
    attn_proj = jnp.dot(attn_low, full_out, preferred_element_type=jnp.float32)
    (resid, normed_mid), mid_back = jax.vjp(middle, token_f32, attn_proj, gains[1], gains[2])
    mid_low = normed_mid.astype(jnp.bfloat16)
    pre = [jnp.dot(mid_low, wide[h], preferred_element_type=jnp.float32) for h in (0, 1)]
    hidden = pre[0].shape[1] // 2
    glu = [jax.vjp(geglu, p[:, :hidden], p[:, hidden:]) for p in pre]
    act_low = jnp.concatenate([act.astype(jnp.bfloat16) for act, _ in glu], axis=1)
    down_out = jnp.dot(act_low, full_down, preferred_element_type=jnp.float32)
    final, tail_back = jax.vjp(partial(finish, live_mask), resid, down_out, gains[3])
    mixed = final.astype(jnp.bfloat16)
    resid_grad, down_grad, final_gain_grad = tail_back(cotangent.astype(jnp.float32))
    down_low = down_grad.astype(jnp.bfloat16)
    grad_down = lead_dot(act_low, down_low).astype(jnp.bfloat16)
    act_grad = tail_dot(down_low, full_down)
    pre_low = []
    for h, (_, glu_back) in enumerate(glu):
        parts = glu_back(act_grad[:, h * hidden : (h + 1) * hidden])
        pre_low.append(jnp.concatenate([g.astype(jnp.bfloat16) for g in parts], axis=1))
    grad_wide = double_dot(mid_low, pre_low)
    mid_grad = tail_dot(pre_low[0], wide[0]) + tail_dot(pre_low[1], wide[1])
    token_grad_mid, attn_grad, post_gain_grad, pre_gain_grad = mid_back((resid_grad, mid_grad))
    attn_grad_low = attn_grad.astype(jnp.bfloat16)
    grad_out = lead_dot(attn_low, attn_grad_low).astype(jnp.bfloat16)
    heads_grad = (
        tail_dot(attn_grad_low, full_out)
        .astype(jnp.bfloat16)
        .reshape(local_rows, HQ, HD)
        .transpose(1, 0, 2)
        .reshape(HQ * local_rows, HD)
    )
    value_grad = lead_dot(probs_low, heads_grad)
    prob_grad = tail_dot(heads_grad, value_low)
    score_grad = (probs * (prob_grad - jnp.sum(probs * prob_grad, axis=-1, keepdims=True))).astype(
        jnp.bfloat16
    )
    query_grad = jnp.dot(score_grad, key_low, preferred_element_type=jnp.float32)
    key_grad = lead_dot(score_grad, query_rows)
    query_grad = query_grad.reshape(HQ, local_rows, HD).transpose(1, 0, 2)
    query_raw_grad, key_raw_grad, query_gain_grad, key_gain_grad = heads_back(
        (query_grad, key_grad)
    )
    query_low_grad = query_raw_grad.astype(jnp.bfloat16)
    key_low_grad = key_raw_grad.astype(jnp.bfloat16)
    value_low_grad = value_grad.astype(jnp.bfloat16)
    blank = jnp.zeros((local_rows, 256), jnp.bfloat16)
    raw_low = pair(query_low_grad, key_low_grad, value_low_grad, blank)
    grad_front = double_dot(input_low, raw_low)
    input_grad = tail_dot(raw_low[0], front[0]) + tail_dot(raw_low[1], front[1])
    token_grad_in, in_gain_grad = input_back(input_grad)
    tokens_grad = (token_grad_mid + token_grad_in).astype(jnp.bfloat16)
    norm_grad = jnp.stack([in_gain_grad, post_gain_grad, pre_gain_grad, final_gain_grad])
    head_grad = jnp.stack([query_gain_grad, key_gain_grad])
    results = reduce(grad_front, grad_out, grad_wide, grad_down, norm_grad, head_grad)
    return (
        mixed,
        tokens_grad,
        results[0],
        results[1],
        results[2],
        results[3],
        results[4],
        results[5],
        results[6],
        results[7],
        results[8],
    )


def norm_forward(values, gain_row):
    scale = lax.rsqrt(jnp.mean(values * values, axis=-1, keepdims=True) + EPSILON)
    unit = values * scale
    return unit, scale, unit * gain_row


def norm_backward(unit, scale, gain_row, grad):
    inner = grad * gain_row
    back = scale * (inner - unit * jnp.mean(inner * unit, axis=-1, keepdims=True))
    return back, jnp.sum(grad * unit, axis=0, keepdims=True)


def head_forward(raw, gain_row, cos_part, sin_part):
    unit, scale, scaled = norm_forward(raw, gain_row)
    lead, second = scaled[:, :128], scaled[:, 128:]
    turned = jnp.concatenate(
        [lead * cos_part - second * sin_part, second * cos_part + lead * sin_part], axis=1
    )
    return unit, scale, turned


def head_backward(unit, scale, gain_row, cos_part, sin_part, grad):
    lead, second = grad[:, :128], grad[:, 128:]
    back = jnp.concatenate(
        [lead * cos_part + second * sin_part, second * cos_part - lead * sin_part], axis=1
    )
    return norm_backward(unit, scale, gain_row, back)


def plain_dot(left, right):
    return jnp.dot(left, right, preferred_element_type=jnp.float32)


def layer_kernel(
    tokens,
    cotangent,
    allowed,
    live,
    cosines,
    sines,
    norms,
    heads,
    front,
    tall,
    wide,
    high,
    mixed,
    tokens_grad,
    front_grad,
    tall_grad,
    wide_grad,
    high_grad,
    norms_grad,
    heads_grad,
    out_full,
    down_full,
    gate_pre,
    up_pre,
    acts,
    total,
):
    low = jnp.bfloat16
    shards = tall.shape[1]

    @pl.loop(0, shards)
    def _(j):
        for h in (0, 1):
            out_full[pl.ds(pl.multiple_of(j * 64 + h * 32, 32), 32), :] = tall[h, j]
            down_full[pl.ds(pl.multiple_of(j * 128 + h * 64, 64), 64), :] = high[h, j]

    gain = [norms[i : i + 1, :] for i in range(4)]
    query_gain, key_gain = heads[0:1, :], heads[1:2, :]
    cos_part, sin_part = cosines[...], sines[...]
    x = tokens[...].astype(jnp.float32)
    in_unit, in_scale, normed = norm_forward(x, gain[0])
    input_low = normed.astype(low)
    raw = [plain_dot(input_low, front[h]) for h in (0, 1)]
    key_raw = jnp.concatenate([raw[0][:, 512:640], raw[1][:, 512:640]], axis=1)
    value_low = jnp.concatenate([raw[0][:, 640:768], raw[1][:, 640:768]], axis=1).astype(low)
    key_unit, key_scale, key_rot = head_forward(key_raw, key_gain, cos_part, sin_part)
    key_low = key_rot.astype(low)
    permit = allowed[...] > 0.5
    kept = []
    outputs = []
    for n in range(HQ):
        query_raw = raw[n // 2][:, n % 2 * HD : n % 2 * HD + HD]
        unit, scale, turned = head_forward(query_raw, query_gain, cos_part, sin_part)
        query_low = (turned * QUERY_SCALE).astype(low)
        scores = jnp.where(permit, tail_dot(query_low, key_low), -1e30)
        expo = jnp.exp(scores - jnp.max(scores, axis=-1, keepdims=True))
        probs = expo / jnp.sum(expo, axis=-1, keepdims=True)
        outputs.append(plain_dot(probs.astype(low), value_low).astype(low))
        kept.append((unit, scale, query_low, probs))
    attn_low = jnp.concatenate(outputs, axis=1)
    post_unit, post_scale, post = norm_forward(plain_dot(attn_low, out_full[...]), gain[1])
    resid = x + post
    mid_unit, mid_scale, mid = norm_forward(resid, gain[2])
    mid_low = mid.astype(low)

    total[...] = jnp.zeros_like(total)
    for h in (0, 1):

        @pl.loop(0, 4)
        def _(i):
            here = pl.multiple_of(i * 256, 256)
            there = pl.multiple_of(h * 1024 + i * 256, 256)
            gate = plain_dot(mid_low, wide[h, :, pl.ds(here, 256)])
            up = plain_dot(mid_low, wide[h, :, pl.ds(pl.multiple_of(1024 + here, 256), 256)])
            bend = jnp.tanh(0.7978845608028654 * (gate + 0.044715 * gate * gate * gate))
            act = (0.5 * gate * (1.0 + bend) * up).astype(low)
            gate_pre[:, pl.ds(there, 256)] = gate
            up_pre[:, pl.ds(there, 256)] = up
            acts[:, pl.ds(there, 256)] = act
            total[...] += plain_dot(act, down_full[pl.ds(there, 256), :])

    last_unit, last_scale, last = norm_forward(total[...], gain[3])
    alive = live[...]
    mixed[...] = ((resid + last) * alive).astype(low)
    out_grad = cotangent[...].astype(jnp.float32) * alive
    down_grad, last_gain = norm_backward(last_unit, last_scale, gain[3], out_grad)
    down_low = down_grad.astype(low)

    total[...] = jnp.zeros_like(total)
    for h in (0, 1):

        @pl.loop(0, 4)
        def _(i):
            here = pl.multiple_of(i * 256, 256)
            beside = pl.multiple_of(1024 + here, 256)
            there = pl.multiple_of(h * 1024 + i * 256, 256)
            gate = gate_pre[:, pl.ds(there, 256)]
            up = up_pre[:, pl.ds(there, 256)]
            act_grad = tail_dot(down_low, down_full[pl.ds(there, 256), :])
            term = lead_dot(acts[:, pl.ds(there, 256)], down_low).astype(low)
            for k in (0, 1):
                for part in (0, 1):
                    start = k * 128 + part * 64
                    high_grad[part, h * 8 + i * 2 + k] = term[start : start + 64]
            square = gate * gate
            bend = jnp.tanh(0.7978845608028654 * gate * (1.0 + 0.044715 * square))
            slope = 0.5 * (1.0 + bend) + 0.5 * gate * (1.0 - bend * bend) * (
                0.7978845608028654 * (1.0 + 0.134145 * square)
            )
            gate_low = (act_grad * up * slope).astype(low)
            up_low = (act_grad * (0.5 * gate * (1.0 + bend))).astype(low)
            wide_grad[h, :, pl.ds(here, 256)] = lead_dot(mid_low, gate_low).astype(low)
            wide_grad[h, :, pl.ds(beside, 256)] = lead_dot(mid_low, up_low).astype(low)
            total[...] += tail_dot(gate_low, wide[h, :, pl.ds(here, 256)]) + tail_dot(
                up_low, wide[h, :, pl.ds(beside, 256)]
            )

    mid_back, mid_gain = norm_backward(mid_unit, mid_scale, gain[2], total[...])
    resid_grad = out_grad + mid_back
    attn_grad, post_gain = norm_backward(post_unit, post_scale, gain[1], resid_grad)
    attn_grad_low = attn_grad.astype(low)
    term = lead_dot(attn_low, attn_grad_low).astype(low)
    for j in range(shards):
        for part in (0, 1):
            tall_grad[part, j] = term[j * 64 + part * 32 : j * 64 + part * 32 + 32]

    value_grad = jnp.zeros((x.shape[0], HD), jnp.float32)
    key_grad = jnp.zeros((x.shape[0], HD), jnp.float32)
    query_gain_grad = jnp.zeros((1, HD), jnp.float32)
    query_grads = []
    for n in range(HQ):
        unit, scale, query_low, probs = kept[n]
        back = tail_dot(attn_grad_low, out_full[n * HD : (n + 1) * HD, :]).astype(low)
        value_grad += lead_dot(probs.astype(low), back)
        prob_grad = tail_dot(back, value_low)
        score_grad = (
            probs * (prob_grad - jnp.sum(probs * prob_grad, axis=-1, keepdims=True))
        ).astype(low)
        key_grad += lead_dot(score_grad, query_low)
        query_grad, gain_term = head_backward(
            unit,
            scale,
            query_gain,
            cos_part,
            sin_part,
            plain_dot(score_grad, key_low) * QUERY_SCALE,
        )
        query_gain_grad += gain_term
        query_grads.append(query_grad.astype(low))
    key_raw_grad, key_gain_grad = head_backward(
        key_unit, key_scale, key_gain, cos_part, sin_part, key_grad
    )
    key_raw_low, value_grad_low = key_raw_grad.astype(low), value_grad.astype(low)
    in_grad = jnp.zeros(x.shape, jnp.float32)
    for h in (0, 1):
        raw_grad = jnp.concatenate(
            query_grads[2 * h : 2 * h + 2]
            + [
                key_raw_low[:, h * 128 : h * 128 + 128],
                value_grad_low[:, h * 128 : h * 128 + 128],
            ],
            axis=1,
        )
        in_grad += tail_dot(raw_grad, front[h, :, 0:768])
        front_grad[h, :, 0:768] = lead_dot(input_low, raw_grad).astype(low)
        front_grad[h, :, 768:896] = jnp.zeros((x.shape[1], 128), low)
    in_back, in_gain = norm_backward(in_unit, in_scale, gain[0], in_grad)
    tokens_grad[...] = (resid_grad + in_back).astype(low)
    for n, row in enumerate((in_gain, post_gain, mid_gain, last_gain)):
        norms_grad[n : n + 1, :] = row
    heads_grad[0:1, :] = query_gain_grad
    heads_grad[1:2, :] = key_gain_grad


def local_fused(
    tokens,
    lengths,
    w_query,
    w_key,
    w_value,
    w_out,
    w_gate,
    w_up,
    w_down,
    norm_gains,
    head_gains,
    cotangent,
):
    rows, width = tokens.shape
    row_index = jnp.arange(rows, dtype=jnp.int32)
    segment, position = layout(lengths[0], row_index)
    live = (segment < 2).astype(jnp.float32)[:, None]
    cos_part, sin_part = angles(position, HD)
    allowed = causal_mask(segment, row_index).astype(jnp.float32)
    front, tall, wide, high, norms, heads = gather_all(
        (w_query, w_key, w_value, w_out, w_gate, w_up, w_down), norm_gains, head_gains
    )
    low = jnp.bfloat16
    vmem = pl.BlockSpec(memory_space=pltpu.VMEM)
    shapes = (
        (tokens.shape, low),
        (tokens.shape, low),
        (front.shape, low),
        (tall.shape, low),
        (wide.shape, low),
        (high.shape, low),
        (norms.shape, jnp.float32),
        (heads.shape, jnp.float32),
    )
    hidden = wide.shape[2]
    results = pl.pallas_call(
        layer_kernel,
        out_shape=tuple(jax.ShapeDtypeStruct(*s) for s in shapes),
        in_specs=[vmem] * 12,
        out_specs=(vmem,) * 8,
        scratch_shapes=[
            pltpu.VMEM((HQ * HD, width), low),
            pltpu.VMEM((hidden, width), low),
            pltpu.VMEM((rows, hidden), jnp.float32),
            pltpu.VMEM((rows, hidden), jnp.float32),
            pltpu.VMEM((rows, hidden), low),
            pltpu.VMEM((rows, width), jnp.float32),
        ],
        compiler_params=pltpu.CompilerParams(vmem_limit_bytes=52 * 1024 * 1024),
        name="layer",
    )(
        tokens,
        cotangent,
        allowed,
        live,
        cos_part,
        sin_part,
        norms.astype(jnp.float32),
        heads.astype(jnp.float32),
        front,
        tall,
        wide,
        high,
    )
    mixed, tokens_grad, grad_front, grad_tall, grad_wide, grad_high, norm_grad, head_grad = results
    return (mixed, tokens_grad) + reduce_all(
        grad_front, grad_tall, grad_wide, grad_high, norm_grad, head_grad
    )


def solution(mesh):
    if mesh.shape["rep"] == 2 and mesh.shape["shard"] == 16:
        step = local_fused
    else:
        step = partial(local, gather_plain, reduce_plain)
    placed = (
        P(("rep", "shard"), None),
        P(("rep", "shard"), None),
        P("shard", None),
        P("shard", None),
        P("shard", None),
        P("shard", None),
        P("shard", None),
        P("shard", None),
        P("shard", None),
        P(None, "shard"),
        P(None, "shard"),
        P(("rep", "shard"), None),
    )
    return jax.shard_map(
        step,
        mesh=mesh,
        in_specs=placed,
        out_specs=(
            P(("rep", "shard"), None),
            P(("rep", "shard"), None),
            P("shard", None),
            P("shard", None),
            P("shard", None),
            P("shard", None),
            P("shard", None),
            P("shard", None),
            P("shard", None),
            P(None, "shard"),
            P(None, "shard"),
        ),
        check_vma=False,
    )
```
